256 devices in a mesh: ctx: 32 (over z, x_lo, core), head: 8 (over y, x_hi).
Axes of the slice: x: 4 (x_hi: 2, x_lo: 2; x = x_hi * 2 + x_lo), y: 4, z: 8, core: 2. Of those that a mesh axis runs over, the one named last changes fastest.
Arguments:
- query_rows: bfloat16 [4096, 32, 128], P('ctx', 'head'), may hold values from -6 to 6, as said below
- key_rows: bfloat16 [4096, 16, 128], P('ctx', 'head'), may hold values from -6 to 6, as said below
- value_rows: bfloat16 [4096, 16, 128], P('ctx', 'head'), may hold values from -6 to 6
- query_tangent: bfloat16 [4096, 32, 128], P('ctx', 'head'), may hold values from -6 to 6
- key_tangent: bfloat16 [4096, 16, 128], P('ctx', 'head'), may hold values from -6 to 6
- value_tangent: bfloat16 [4096, 16, 128], P('ctx', 'head'), may hold values from -6 to 6
- curvature: float32 [32, 4096], P('head', 'ctx'), may hold values from 0.5 to 8192, as said below
- documents: int32 [4096], P('ctx'), may hold values from 0 to 7, never falling along the last dimension, each value on 1 to 2048 neighbouring positions
Outputs:
- query_grad: bfloat16 [4096, 32, 128], P('ctx', 'head')
- key_grad: bfloat16 [4096, 16, 128], P('ctx', 'head')
- value_grad: bfloat16 [4096, 16, 128], P('ctx', 'head')
- doc_scores: float32 [8], replicated
The draws below stay inside these ranges and needn't reach their ends.
Inputs may be any that keep to these rules, and one draw needn't show every extreme that they name: `query_rows`: finite entries. `key_rows`: finite entries. `curvature`: positive entries.
All inputs are finite; a program needn't handle non-finite values.
Results may differ from the reference program's by a relative error of at most 0.019.
Values may be sent and summed in bfloat16 or wider, within the bound.
No kernel may reach another device: no remote copies, remote signals or barrier semaphores. Data moves between devices by JAX's collectives and lax.ppermute only.
A program may use at most 64 MiB of HBM per device.

```python
import math
import jax
import jax.numpy as jnp
import numpy as np
from jax import lax

H = 32
KVH = 16
HD = 128
DOCS = 8
TOKENS = 4096


def draw_query_rows(key, part):
    key = jax.random.fold_in(key, 11)
    field = jnp.clip(jax.random.normal(key, (TOKENS, H, HD), jnp.float32), -4.0, 4.0)
    return field.astype(jnp.bfloat16)


def draw_key_rows(key, part):
    key = jax.random.fold_in(key, 13)
    field = jnp.clip(jax.random.normal(key, (TOKENS, KVH, HD), jnp.float32), -4.0, 4.0)
    return field.astype(jnp.bfloat16)


def draw_curvature(key, part):
    key = jax.random.fold_in(key, 17)
    places = jnp.arange(TOKENS, dtype=jnp.float32) + 1.0
    factor = jnp.exp(jax.random.uniform(key, (H, TOKENS), jnp.float32, math.log(0.5), math.log(2.0)))
    return factor * places[None, :]


def steps_of(rng, dims, shards, least, high):
    factor_of = 1.0
    for dim, blocks in shards:
        draws = jax.random.uniform(jax.random.fold_in(jax.random.fold_in(rng, 6), dim), (blocks,), jnp.float32, least / len(shards), high / len(shards))
        factor_of = factor_of * jnp.repeat(jnp.exp(draws), dims[dim] // blocks).reshape((-1,) + (1,) * (len(dims) - 1 - dim))
    return factor_of


def profile(number_of, total, most, slope):
    weights = [(1 << 20) // math.isqrt(standing ** slope) + 1 for standing in range(2, number_of + 1)]
    rest, given = total - most - (number_of - 1), [1] * (number_of - 1)
    while rest > 0:
        movable = [i for i in range(number_of - 1) if given[i] < most]
        pool, remaining = sum([weights[i] for i in movable]), rest
        for i in movable:
            addition = min(most - given[i], max(1, remaining * weights[i] // pool), rest)
            given[i] = given[i] + addition
            rest = rest - addition
    return np.array([most] + given)


def ragged(rng, amount, total, limit, slope):
    if amount == 2:
        one = jax.random.randint(rng, (), max(1, total - limit), min(limit, total - 1) + 1)
        return jnp.stack([one, total - one])
    sizes = jnp.asarray(profile(amount, total, limit, slope), jnp.int32)
    pairs = (amount - 1) // 2
    donor, taker = sizes[1:1 + 2 * pairs:2], sizes[2:2 + 2 * pairs:2]
    slack = jnp.minimum(donor - 1, limit - taker)
    passed = jax.random.randint(jax.random.fold_in(rng, 1), (pairs,), 0, 1 << 20) % (slack + 1)
    sizes = sizes.at[1:1 + 2 * pairs:2].set(donor - passed).at[2:2 + 2 * pairs:2].set(taker + passed)
    return sizes[jax.random.permutation(jax.random.fold_in(rng, 2), amount)]


def noise(key, dims, scale, most, split=(), kind=jnp.bfloat16):
    entries = scale * jax.random.normal(key, dims, jnp.float32)
    if split:
        entries = entries * steps_of(key, dims, split, -0.22, 0.18)
    return jnp.clip(entries, -most, most).astype(kind)


def setup_inputs(seed: int = 0) -> dict:
    seeds = jax.random.split(jax.random.key(seed), 9)
    return {
        "query_rows": draw_query_rows(jax.random.fold_in(seeds[8], 71), 0),
        "key_rows": draw_key_rows(jax.random.fold_in(seeds[8], 71), 0),
        "value_rows": noise(seeds[2], (TOKENS, KVH, HD), 1.0, 6.0, ((0, 32), (1, 8))),
        "query_tangent": noise(seeds[3], (TOKENS, H, HD), 1.0, 6.0, ((0, 32), (1, 8))),
        "key_tangent": noise(seeds[4], (TOKENS, KVH, HD), 1.0, 6.0, ((0, 32), (1, 8))),
        "value_tangent": noise(seeds[5], (TOKENS, KVH, HD), 1.0, 6.0, ((0, 32), (1, 8))),
        "curvature": draw_curvature(jax.random.fold_in(seeds[8], 71), 0),
        "documents": jnp.searchsorted(jnp.cumsum(ragged(seeds[7], DOCS, TOKENS, TOKENS // 2, 2)), jnp.arange(TOKENS), side="right").astype(jnp.int32),
    }


score_scale = 1.0 / 12.0


def one_group(inputs):
    queries, key_block, value_block, query_tan, key_tan, value_tan, curv_rows = inputs
    row_count = key_block.shape[0]
    places = lax.iota(jnp.int32, row_count)
    allowed = places[None, :] <= places[:, None]
    key_grad = jnp.zeros(key_block.shape, jnp.float32)
    value_grad = jnp.zeros(value_block.shape, jnp.float32)
    query_grads = []
    for member in range(queries.shape[0]):
        qpart = queries[member]
        scores = jnp.dot(qpart, key_block.T, preferred_element_type=jnp.float32) * score_scale
        maxima = jnp.max(jnp.where(allowed, scores, -jnp.inf), axis=1)
        weights = jnp.where(allowed, jnp.exp(scores - maxima[:, None]), 0.0)
        totals = jnp.sum(weights, axis=1)
        slopes = (jnp.dot(query_tan[member], key_block.T, preferred_element_type=jnp.float32)
                  + jnp.dot(qpart, key_tan.T, preferred_element_type=jnp.float32)) * score_scale
        weighted = weights * slopes
        spreads = jnp.sum(weighted, axis=1)
        weights_low = weights.astype(jnp.bfloat16)
        outputs = jnp.dot(weights_low, value_block, preferred_element_type=jnp.float32) / totals[:, None]
        out_tan = (jnp.dot(weighted.astype(jnp.bfloat16), value_block, preferred_element_type=jnp.float32)
                   + jnp.dot(weights_low, value_tan, preferred_element_type=jnp.float32)) / totals[:, None]
        out_tan = out_tan - (spreads / totals)[:, None] * outputs
        cotangent = (curv_rows[member][:, None] * out_tan).astype(jnp.bfloat16)
        log_totals = maxima + jnp.log(totals)
        probability = jnp.where(allowed, jnp.exp(scores - log_totals[:, None]), 0.0)
        pushed = jnp.dot(cotangent, value_block.T, preferred_element_type=jnp.float32)
        deltas = jnp.sum(cotangent.astype(jnp.float32) * outputs, axis=1)
        grad_scores = probability * (pushed - deltas[:, None])
        low_grad = grad_scores.astype(jnp.bfloat16)
        query_grads.append(jnp.dot(low_grad, key_block, preferred_element_type=jnp.float32) * score_scale)
        key_grad = key_grad + jnp.dot(low_grad.T, qpart, preferred_element_type=jnp.float32) * score_scale
        value_grad = value_grad + jnp.dot(probability.astype(jnp.bfloat16).T, cotangent,
                                          preferred_element_type=jnp.float32)
    return jnp.stack(query_grads), key_grad, value_grad


def reference(query_rows, key_rows, value_rows, query_tangent, key_tangent, value_tangent, curvature, documents):
    group_size = H // KVH
    stacked_q = jnp.transpose(query_rows.reshape(TOKENS, KVH, group_size, HD), (1, 2, 0, 3))
    stacked_qt = jnp.transpose(query_tangent.reshape(TOKENS, KVH, group_size, HD), (1, 2, 0, 3))
    stacked_k = jnp.transpose(key_rows, (1, 0, 2))
    stacked_v = jnp.transpose(value_rows, (1, 0, 2))
    stacked_kt = jnp.transpose(key_tangent, (1, 0, 2))
    stacked_vt = jnp.transpose(value_tangent, (1, 0, 2))
    stacked_c = curvature.reshape(KVH, group_size, TOKENS)
    query_part, key_part, value_part = lax.map(
        one_group, (stacked_q, stacked_k, stacked_v, stacked_qt, stacked_kt, stacked_vt, stacked_c))
    query_grad = jnp.transpose(query_part, (2, 0, 1, 3)).reshape(TOKENS, H, HD)
    key_grad = jnp.transpose(key_part, (1, 0, 2))
    value_grad = jnp.transpose(value_part, (1, 0, 2))
    token_terms = (jnp.sum(query_tangent.astype(jnp.float32) * query_grad, axis=(1, 2))
                   + jnp.sum(key_tangent.astype(jnp.float32) * key_grad, axis=(1, 2))
                   + jnp.sum(value_tangent.astype(jnp.float32) * value_grad, axis=(1, 2)))
    onehot = (documents[:, None] == lax.iota(jnp.int32, DOCS)[None, :]).astype(jnp.float32)
    doc_sums = jnp.dot(token_terms, onehot, precision=lax.Precision.HIGHEST)
    counts = jnp.sum(onehot, axis=0)
    doc_scores = doc_sums / (counts * (H * HD))
    return (query_grad.astype(jnp.bfloat16), key_grad.astype(jnp.bfloat16),
            value_grad.astype(jnp.bfloat16), doc_scores)
```

```python
import jax
import jax.numpy as jnp
from jax import lax
from jax.experimental import pallas as pl
from jax.experimental.pallas import tpu as pltpu
from jax.sharding import Mesh, PartitionSpec as P

DOCS = 8
NZ = 8
ROWS = 128
HD = 128
CH = 2 * ROWS
MQ = 2 * CH
BK = 2 * CH
SCALE = 1.0 / 12.0
LOWEST = -1e30
ALL = ("z", "xl", "c", "h")
BF = jnp.bfloat16
F32 = jnp.float32


def dot_nt(a, b):
    return lax.dot_general(a, b, (((1,), (1,)), ((), ())), preferred_element_type=F32)


def dot_nn(a, b):
    return lax.dot_general(a, b, (((1,), (0,)), ((), ())), preferred_element_type=F32)


def dot_tn(a, b):
    return lax.dot_general(a, b, (((0,), (0,)), ((), ())), preferred_element_type=F32)


def attention_kernel(*refs):
    at_ref, q_ref, curv_ref = refs[:3]
    chunks = refs[3 : 3 + 2 * NZ]
    gq_ref, gkv_ref = refs[3 + 2 * NZ : 5 + 2 * NZ]
    kv, score, acc_v, acc_t, top, tot, spr, sems = refs[5 + 2 * NZ :]
    z = at_ref[0]
    core = at_ref[1]

    def copy_of(d, side):
        return pltpu.make_async_copy(
            chunks[side * NZ + d], kv.at[d, pl.ds(side * CH, CH)], sems.at[d, side]
        )

    for d in range(NZ):
        for side in range(2):
            copy_of(d, side).start()

    def wait_for(d):
        for side in range(2):
            pltpu.make_async_copy(
                kv.at[d, pl.ds(side * CH, CH)], kv.at[d, pl.ds(side * CH, CH)], sems.at[d, side]
            ).wait()

    def forward(d, diagonal):
        wait_for(d)
        s = dot_nt(q_ref[:, HD:], kv[d, :, :HD])
        slope = dot_nt(q_ref[...], kv[d, :, : 2 * HD])
        if diagonal:
            row = lax.broadcasted_iota(jnp.int32, (MQ, BK), 0) % CH
            col = lax.broadcasted_iota(jnp.int32, (MQ, BK), 1)
            row_pos = (row // ROWS) * CH + core * ROWS + row % ROWS
            col_core = jnp.where(col >= CH, 1 - core, core)
            col = col % CH
            col_pos = (col // ROWS) * CH + col_core * ROWS + col % ROWS
            s = jnp.where(col_pos <= row_pos, s, LOWEST)
        score[d] = s
        block_top = jnp.max(s, axis=1, keepdims=True)
        if diagonal:
            new_top = block_top
        else:
            new_top = jnp.maximum(top[...], block_top)
        e = jnp.exp((s - new_top) * SCALE)
        f = e * (slope * SCALE)
        part_v = dot_nn(e.astype(BF), kv[d, :, 2 * HD :])
        part_t = dot_nn(f.astype(BF), kv[d, :, 2 * HD : 3 * HD])
        sum_e = jnp.sum(e, axis=1, keepdims=True)
        sum_f = jnp.sum(f, axis=1, keepdims=True)
        if diagonal:
            acc_v[...] = part_v
            acc_t[...] = part_t
            tot[...] = sum_e
            spr[...] = sum_f
        else:
            factor = jnp.exp((top[...] - new_top) * SCALE)
            acc_v[...] = acc_v[...] * factor + part_v
            acc_t[...] = acc_t[...] * factor + part_t
            tot[...] = tot[...] * factor + sum_e
            spr[...] = spr[...] * factor + sum_f
        top[...] = new_top

    forward(0, True)

    @pl.loop(1, z + 1)
    def _(d):
        forward(d, False)

    @pl.loop(z + 1, NZ)
    def _(d):
        wait_for(d)

    inv = 1.0 / tot[...]
    out = acc_v[:, :HD] * inv
    out_tan = (acc_t[...] + acc_v[:, HD:]) * inv - (spr[...] * inv) * out
    cot = (curv_ref[...] * out_tan).astype(BF)
    log_tot = top[...] * SCALE + jnp.log(tot[...])
    delta = jnp.sum(cot.astype(F32) * out, axis=1, keepdims=True)
    acc_t[...] = jnp.zeros((MQ, HD), F32)

    @pl.loop(0, z + 1)
    def _(d):
        p = jnp.exp(score[d] * SCALE - log_tot)
        g = p * (dot_nt(cot, kv[d, :, 2 * HD : 3 * HD]) - delta)
        gb = g.astype(BF)
        acc_t[...] += dot_nn(gb, kv[d, :, :HD])
        gkv_ref[d, :, :HD] = (dot_tn(gb, q_ref[:, HD:]) * SCALE).astype(BF)
        gkv_ref[d, :, HD:] = dot_tn(p.astype(BF), cot).astype(BF)

    @pl.loop(z + 1, NZ)
    def _(d):
        gkv_ref[d] = jnp.zeros((BK, 2 * HD), BF)

    gq_ref[...] = (acc_t[...] * SCALE).astype(BF)


def attention(at, q, curv, chunks):
    vmem = pl.BlockSpec(memory_space=pltpu.VMEM)
    return pl.pallas_call(
        attention_kernel,
        out_shape=(
            jax.ShapeDtypeStruct((MQ, HD), BF),
            jax.ShapeDtypeStruct((NZ, BK, 2 * HD), BF),
        ),
        in_specs=[pl.BlockSpec(memory_space=pltpu.SMEM), vmem, vmem]
        + [pl.BlockSpec(memory_space=pl.ANY)] * (2 * NZ),
        out_specs=(vmem, vmem),
        scratch_shapes=[
            pltpu.VMEM((NZ, BK, 4 * HD), BF),
            pltpu.VMEM((NZ, MQ, BK), F32),
            pltpu.VMEM((MQ, 2 * HD), F32),
            pltpu.VMEM((MQ, HD), F32),
            pltpu.VMEM((MQ, 1), F32),
            pltpu.VMEM((MQ, 1), F32),
            pltpu.VMEM((MQ, 1), F32),
            pltpu.SemaphoreType.DMA((NZ, 2)),
        ],
        compiler_params=pltpu.CompilerParams(vmem_limit_bytes=48 * 1024 * 1024),
        cost_estimate=pl.CostEstimate(
            flops=8 * 2 * MQ * 4096 * 256, bytes_accessed=8 << 20, transcendentals=2 * MQ * 4096
        ),
    )(at, q, curv, *chunks)


def swap(x, axis):
    return lax.ppermute(x, axis, [(0, 1), (1, 0)])


def around(x, step):
    return lax.ppermute(x, "z", [(i, (i + step) % NZ) for i in range(NZ)])


def pick(x, index, axis):
    return lax.dynamic_index_in_dim(x, index, axis, keepdims=False)


def on_device(
    query_rows,
    key_rows,
    value_rows,
    query_tangent,
    key_tangent,
    value_tangent,
    curvature,
    documents,
):
    z = lax.axis_index("z")
    xl = lax.axis_index("xl")
    core = lax.axis_index("c")
    kv_all = jnp.concatenate([key_rows, key_tangent, value_rows, value_tangent], axis=-1)
    q_all = jnp.concatenate([query_tangent, query_rows], axis=-1).reshape(ROWS, 2, 4 * HD)
    curv_all = curvature.reshape(2, 2, ROWS)
    both = jnp.concatenate([kv_all, q_all], axis=0)
    mine = pick(both, xl, 1)
    other = swap(pick(both, 1 - xl, 1), "xl")
    curv_mine = pick(curv_all, xl, 0)
    curv_other = swap(pick(curv_all, 1 - xl, 0), "xl")

    def ordered(a, b):
        return jnp.where(xl == 0, a, b), jnp.where(xl == 0, b, a)

    low, high = ordered(mine, other)
    chunk = jnp.concatenate([low[:ROWS], high[:ROWS]], axis=0)
    q = jnp.concatenate([low[ROWS:], high[ROWS:]], axis=0)
    q = jnp.concatenate([q[:, : 2 * HD], q[:, 2 * HD :]], axis=0)
    low_c, high_c = ordered(curv_mine, curv_other)
    curv = jnp.concatenate([low_c, high_c], axis=1).reshape(MQ, 1)

    chunks = [None] * NZ
    chunks[0] = chunk
    ahead = behind = chunk
    for step in range(1, NZ // 2):
        ahead = around(ahead, 1)
        behind = around(behind, -1)
        chunks[step] = ahead
        chunks[NZ - step] = behind
    chunks[NZ // 2] = jnp.concatenate([around(ahead[:ROWS], 1), around(behind[ROWS:], -1)], axis=0)
    sibling = [swap(c, "c") for c in chunks]

    at = jnp.stack([z, core])
    gq, gkv = attention(at, q, curv, chunks + sibling)

    gq = gq.reshape(2, 2, ROWS, HD)
    gq_other = swap(pick(gq, 1 - xl, 1), "xl")
    gq_mine = pick(gq, xl, 1)
    gq_low, gq_high = ordered(gq_mine, gq_other)
    query_grad = jnp.transpose(jnp.concatenate([gq_low, gq_high], axis=0), (1, 0, 2))

    from_sibling = swap(gkv[:, CH:], "c")
    part = (gkv[:, :CH].astype(F32) + from_sibling.astype(F32)).astype(BF)
    target = lax.rem(z - lax.iota(jnp.int32, NZ) + NZ, NZ)
    part = jnp.take(part, target, axis=0)
    part = part.reshape(2 * NZ * ROWS, 2 * HD)
    part = lax.all_to_all(part, ("z", "xl"), 0, 0, tiled=True)
    grads = jnp.sum(part.reshape(NZ, 2, ROWS, 2 * HD).astype(F32), axis=0)
    grads = jnp.transpose(grads, (1, 0, 2))
    key_grad = grads[..., :HD]
    value_grad = grads[..., HD:]

    token_terms = (
        jnp.sum(query_tangent.astype(F32) * query_grad.astype(F32), axis=(1, 2))
        + jnp.sum(key_tangent.astype(F32) * key_grad, axis=(1, 2))
        + jnp.sum(value_tangent.astype(F32) * value_grad, axis=(1, 2))
    )
    onehot = (documents[:, None] == lax.iota(jnp.int32, DOCS)[None, :]).astype(F32)
    doc_sums = jnp.sum(token_terms[:, None] * onehot, axis=0)
    counts = jnp.sum(onehot, axis=0)
    terms = jnp.concatenate([doc_sums, counts])
    world = NZ * 2 * 2 * 8
    spread = lax.all_to_all(jnp.tile(terms, world), ALL, 0, 0, tiled=True)
    doc_sums, counts = jnp.split(jnp.sum(spread.reshape(world, 2 * DOCS), axis=0), 2)
    doc_scores = doc_sums / (counts * (4 * HD))
    return (query_grad, key_grad.astype(BF), value_grad.astype(BF), doc_scores)


def solution(mesh):
    split = Mesh(mesh.devices.reshape(NZ, 2, 2, 8), ALL)
    ctx = ("z", "xl", "c")
    rows = P(ctx, "h", None)
    in_specs = (rows,) * 6 + (P("h", ctx), P(ctx))
    out_specs = (rows, rows, rows, P())
    return jax.shard_map(
        on_device, mesh=split, in_specs=in_specs, out_specs=out_specs, check_vma=False
    )
```

```python
import math

import jax
import jax.numpy as jnp
from jax import lax
from jax.experimental import pallas as pl
from jax.experimental.pallas import tpu as pltpu
from jax.sharding import Mesh, PartitionSpec as P

DOCS = 8
NZ = 8
FAR = NZ // 2
ROWS = 128
HD = 128
DR = 16
PIECE = ROWS + DR
CH = 2 * ROWS
MQ = 2 * CH
BK = 2 * CH
SCALE = 1.0 / 12.0
SCALE2 = SCALE * math.log2(math.e)
LOWEST = -1e30
ALL = ("z", "xl", "c", "h")
BF = jnp.bfloat16
F32 = jnp.float32
VMEM_LIMIT = 28 * 1024 * 1024


def dot(a, b):
    return lax.dot_general(a, b, (((1,), (0,)), ((), ())), preferred_element_type=F32)


def whole_call(kernel, out_shape, *arrays, limit=None):
    vmem = pl.BlockSpec(memory_space=pltpu.VMEM)
    return pl.pallas_call(
        kernel,
        out_shape=out_shape,
        in_specs=[vmem] * len(arrays),
        out_specs=(vmem,) * len(out_shape),
        compiler_params=pltpu.CompilerParams(vmem_limit_bytes=limit),
        cost_estimate=pl.CostEstimate(flops=0, bytes_accessed=1 << 20, transcendentals=0),
    )(*arrays)


def pack_keys_kernel(k, v, kt, vt, docs, kv_mine, kv_other):
    first = lax.axis_index("xl") == 0
    ids = jnp.broadcast_to(docs[...], (DR, HD)).astype(F32).astype(BF)
    for col, ref in enumerate((k, kt, v, vt)):
        a, b = ref[:, 0, :], ref[:, 1, :]
        lanes = pl.ds(col * HD, HD)
        kv_mine[pl.ds(0, ROWS), lanes] = jnp.where(first, a, b)
        kv_other[pl.ds(0, ROWS), lanes] = jnp.where(first, b, a)
        kv_mine[pl.ds(ROWS, DR), lanes] = ids
        kv_other[pl.ds(ROWS, DR), lanes] = ids


def pack_queries_kernel(q, qt, curv, q_mine, q_other):
    first = lax.axis_index("xl") == 0
    for h in range(2):
        for col, ref in enumerate((qt, q)):
            a, b = ref[:, h, :], ref[:, 2 + h, :]
            lanes = pl.ds((2 * h + col) * HD, HD)
            q_mine[pl.ds(0, ROWS), lanes] = jnp.where(first, a, b)
            q_other[pl.ds(0, ROWS), lanes] = jnp.where(first, b, a)
        a, b = curv[pl.ds(h, 1)], curv[pl.ds(2 + h, 1)]
        lanes = pl.ds(2 * h * HD, HD)
        for ref, row in ((q_mine, jnp.where(first, a, b)), (q_other, jnp.where(first, b, a))):
            row = jnp.broadcast_to(row, (DR, HD))
            line = lax.broadcasted_iota(jnp.int32, (DR, HD), 0)
            high = row.astype(BF).astype(F32)
            rest = row - high
            mid = rest.astype(BF).astype(F32)
            parts = jnp.where(line == 0, high, jnp.where(line == 1, mid, rest - mid))
            ref[pl.ds(ROWS, DR), lanes] = jnp.where(line < 3, parts, 0.0).astype(BF)
            ref[pl.ds(ROWS, DR), pl.ds((2 * h + 1) * HD, HD)] = jnp.zeros((DR, HD), BF)


def grads_kernel(parts, key_grad, value_grad):
    for head in range(2):
        total = parts[head].astype(F32)
        for z in range(1, NZ):
            total += parts[2 * z + head].astype(F32)
        key_grad[:, head, :] = total[:, :HD].astype(BF)
        value_grad[:, head, :] = total[:, HD:].astype(BF)


def query_grads_kernel(mine, other, query_grad):
    first = lax.axis_index("xl") == 0
    for h in range(2):
        query_grad[:, h, :] = jnp.where(first, mine[h], other[h])
        query_grad[:, 2 + h, :] = jnp.where(first, other[h], mine[h])


def rows_of(h, s):
    return (h * 2 + s) * ROWS


def masked(scores, xl, core):
    key = lax.broadcasted_iota(jnp.int32, scores.shape, 0)
    row = lax.broadcasted_iota(jnp.int32, scores.shape, 1) % CH
    row_xl = jnp.where(row >= ROWS, 1 - xl, xl)
    row_pos = row_xl * CH + core * ROWS + row % ROWS
    key_core = jnp.where(key >= CH, 1 - core, core)
    key = key % CH
    key_xl = jnp.where(key >= ROWS, 1 - xl, xl)
    key_pos = key_xl * CH + key_core * ROWS + key % ROWS
    return jnp.where(key_pos <= row_pos, scores, LOWEST)


def folded(x, combine):
    return combine(x.reshape(x.shape[0] // 8, 8, x.shape[1]), axis=0)


A0, B0, A1, B1, A2, B2, A3, B3, N4 = range(9)
XA1, XB1, XA2, XB2, XA3, XB3, X4 = range(9, 16)
NS = 16
BLOCKS = ((A0, B0), (A1, B1), (A2, B2), (A3, B3), (N4, X4), (XA3, XB3), (XA2, XB2), (XA1, XB1))


def pieces_of(n):
    out = []
    for side in range(2):
        for at in BLOCKS[n]:
            flip = at >= XA1
            out.append((at, PIECE * (1 - side if flip else side)))
    return out


def attention_kernel(*refs):
    q_refs = refs[:2]
    sources = refs[2 : 2 + NS]
    refs = refs[2 + NS :]
    gq_mine, gq_other, g_own, g_sib, doc_ref, count_ref = refs[:6]
    q_t, q_n, score, acc_v, acc_t, cot_t, cot_n, stat, tops, tots, sprs, doc_acc = refs[6:]
    z = lax.axis_index("z")
    xl = lax.axis_index("xl")
    core = lax.axis_index("c")

    def keys(n, first, last):
        return jnp.concatenate(
            [
                sources[at][row : row + ROWS, first * HD : last * HD]
                for at, row in pieces_of(n)
            ],
            axis=0,
        )

    def onehot(piece):
        at, row = piece
        ids = sources[at][row + ROWS : row + PIECE, :HD].astype(F32).astype(jnp.int32)
        names = lax.broadcasted_iota(jnp.int32, (DR, ROWS), 0)
        return jnp.where(ids == names, 1.0, 0.0)

    def place(n):
        return jnp.where(core == 0, n, NZ - n) if n else 0

    def before(block):
        for n in range(1, NZ):
            pl.when(z >= place(n))(lambda n=n: block(n))

    curv = []
    for h in range(2):
        for s in range(2):
            q = q_refs[s]
            x = q[:ROWS, 2 * h * HD : 2 * (h + 1) * HD]
            q_n[pl.ds(rows_of(h, s), ROWS)] = x
            q_t[:, pl.ds(rows_of(h, s), ROWS)] = x.T
            line = q[ROWS:, 2 * h * HD : (2 * h + 1) * HD].astype(F32)
            curv.append(jnp.sum(line, axis=0, keepdims=True))
    curv = jnp.concatenate(curv, axis=1)

    def scores_of(d, diagonal):
        s = dot(keys(d, 0, 1), q_t[HD:, :])
        if diagonal:
            s = masked(s, xl, core)
        score[d] = s
        top = folded(s, jnp.max)
        tops[...] = top if diagonal else jnp.maximum(tops[...], top)

    scores_of(0, True)
    before(lambda d: scores_of(d, False))
    top = jnp.max(tops[...], axis=0, keepdims=True) * SCALE2
    stat[0:1, :] = top

    def forward(d, diagonal):
        values_t = keys(d, 2, 4).T
        slope = dot(keys(d, 0, 2), q_t[...])
        e = jnp.exp2(score[d] * SCALE2 - stat[0:1, :])
        f = e * slope
        part_v = dot(values_t, e.astype(BF))
        part_t = dot(values_t[:HD], f.astype(BF))
        tot, spr = folded(e, jnp.sum), folded(f, jnp.sum)
        if diagonal:
            acc_v[...], acc_t[...], tots[...], sprs[...] = part_v, part_t, tot, spr
        else:
            acc_v[...] += part_v
            acc_t[...] += part_t
            tots[...] += tot
            sprs[...] += spr

    forward(0, True)
    before(lambda d: forward(d, False))

    tot = jnp.sum(tots[...], axis=0, keepdims=True)
    spr = jnp.sum(sprs[...], axis=0, keepdims=True) * SCALE
    inv = 1.0 / tot
    out = acc_v[:HD, :] * inv
    out_tan = (acc_t[...] * SCALE + acc_v[HD:, :]) * inv - (spr * inv) * out
    cot = (curv * out_tan).astype(BF)
    cot_t[...] = cot
    cot_n[...] = cot.T
    stat[1:2, :] = stat[0:1, :] + jnp.log2(tot)
    stat[2:3, :] = jnp.sum(cot.astype(F32) * out, axis=0, keepdims=True)
    acc_t[...] = jnp.zeros((HD, MQ), F32)
    doc_acc[...] = jnp.zeros((DR, HD), F32)

    def by_document(hots, terms):
        hot = jnp.concatenate(hots, axis=1).astype(BF)
        high = terms.astype(BF)
        low = (terms - high.astype(F32)).astype(BF)
        return dot(hot, high) + dot(hot, low)

    def backward(d):
        keys_t = keys(d, 0, 1).T
        p = jnp.exp2(score[d] * SCALE2 - stat[1:2, :])
        push = dot(keys(d, 2, 3), cot_t[...])
        g = (p * (push - stat[2:3, :])).astype(BF)
        acc_t[...] += dot(keys_t, g)
        gk = dot(g, q_n[:, HD:]) * SCALE
        gv = dot(p.astype(BF), cot_n[...])
        terms = gk * keys(d, 1, 2).astype(F32) + gv * keys(d, 3, 4).astype(F32)
        for side, g_ref in enumerate((g_own, g_sib)):
            for s in range(2):
                at = side * CH + s * ROWS
                to_xl = xl if s == 0 else 1 - xl
                if d == FAR:
                    to_xl = jnp.where(core == 0, to_xl, 1 - to_xl)
                g_ref[z - place(d), to_xl, :, :HD] = gk[at : at + ROWS].astype(BF)
                g_ref[z - place(d), to_xl, :, HD:] = gv[at : at + ROWS].astype(BF)
        doc_acc[...] += by_document([onehot(p) for p in pieces_of(d)], terms)

    backward(0)
    before(backward)

    @pl.loop(z + 1, NZ)
    def _(to):
        g_own[to] = jnp.zeros((2, ROWS, 2 * HD), BF)
        g_sib[to] = jnp.zeros((2, ROWS, 2 * HD), BF)

    counts = sum(onehot(p) for n in range(NZ) for p in pieces_of(n))
    count_ref[...] = jnp.broadcast_to(jnp.sum(counts, axis=1, keepdims=True), (DR, ROWS))
    gq = (acc_t[...] * SCALE).T
    terms = gq * q_n[:, :HD].astype(F32)
    hots = [onehot(p) for p in pieces_of(0)[:2]]
    doc = doc_acc[...] + by_document(hots * 2, terms)
    for h in range(2):
        for s, ref in enumerate((gq_mine, gq_other)):
            ref[h] = gq[rows_of(h, s) : rows_of(h, s) + ROWS].astype(BF)
    doc_ref[...] = jnp.broadcast_to(jnp.sum(doc, axis=1, keepdims=True), (DR, HD))


def attention(q, sources):
    vmem = pl.BlockSpec(memory_space=pltpu.VMEM)
    gq_shape = jax.ShapeDtypeStruct((2, ROWS, HD), BF)
    g_shape = jax.ShapeDtypeStruct((NZ, 2, ROWS, 2 * HD), BF)
    line_shape = jax.ShapeDtypeStruct((DR, HD), F32)
    return pl.pallas_call(
        attention_kernel,
        out_shape=(gq_shape, gq_shape, g_shape, g_shape, line_shape, line_shape),
        in_specs=[vmem] * (2 + len(sources)),
        out_specs=(vmem,) * 6,
        scratch_shapes=[
            pltpu.VMEM((2 * HD, MQ), BF),
            pltpu.VMEM((MQ, 2 * HD), BF),
            pltpu.VMEM((NZ, BK, MQ), F32),
            pltpu.VMEM((2 * HD, MQ), F32),
            pltpu.VMEM((HD, MQ), F32),
            pltpu.VMEM((HD, MQ), BF),
            pltpu.VMEM((MQ, HD), BF),
            pltpu.VMEM((8, MQ), F32),
            pltpu.VMEM((8, MQ), F32),
            pltpu.VMEM((8, MQ), F32),
            pltpu.VMEM((8, MQ), F32),
            pltpu.VMEM((DR, HD), F32),
        ],
        compiler_params=pltpu.CompilerParams(vmem_limit_bytes=VMEM_LIMIT),
        cost_estimate=pl.CostEstimate(
            flops=8 * 2 * MQ * 4096 * 256, bytes_accessed=8 << 20, transcendentals=2 * MQ * 4096
        ),
    )(*q, *sources)


def swap(x, axis):
    return lax.ppermute(x, axis, [(0, 1), (1, 0)])


def around(x):
    pairs = [(2 * i + c, 2 * ((i + step) % NZ) + c) for i in range(NZ) for c, step in ((0, 1), (1, -1))]
    return lax.ppermute(x, ("z", "c"), pairs)


def bundle(x):
    return jnp.concatenate([x, swap(x, "c")], axis=0)


def sum_of_four(x, axes, size, one, two):
    got = [
        lax.ppermute(x, axes, [(i, i ^ m) for i in range(size)]) for m in (one, two, one ^ two)
    ]
    return (x + got[0]) + (got[1] + got[2])


def on_device(
    query_rows,
    key_rows,
    value_rows,
    query_tangent,
    key_tangent,
    value_tangent,
    curvature,
    documents,
):
    piece = jax.ShapeDtypeStruct((PIECE, 4 * HD), BF)
    kv_mine, kv_other = whole_call(
        pack_keys_kernel, (piece, piece),
        key_rows, value_rows, key_tangent, value_tangent, documents.reshape(1, ROWS),
    )
    kv_other = swap(kv_other, "xl")
    a = [bundle(kv_mine)]
    a[0], query_rows = lax.optimization_barrier((a[0], query_rows))
    a.append(around(a[0]))
    q_mine, q_other = whole_call(
        pack_queries_kernel, (piece, piece), query_rows, query_tangent, curvature
    )
    kv_other, q_other = lax.optimization_barrier((kv_other, q_other))
    b = [bundle(kv_other)]
    b.append(around(b[0]))
    crossed = []
    for k in range(1, FAR):
        late_a, b[k], q_other = lax.optimization_barrier((a[k], b[k], q_other))
        if k == 1:
            q_other = swap(q_other, "xl")
        crossed.append(swap(late_a, "c"))
        if k < FAR - 1:
            a.append(around(a[k]))
            late_b, _ = lax.optimization_barrier((b[k], a[k + 1]))
            crossed.append(swap(late_b, "c"))
            b.append(around(b[k]))
    crossed.append(swap(b[FAR - 1], "c"))
    far = around(jnp.where(lax.axis_index("c") == 0, a[FAR - 1], b[FAR - 1]))
    native = [x for pair in zip(a, b) for x in pair]
    gq_mine, gq_other, g_own, g_sib, doc, count = attention(
        (q_mine, q_other), native + [far] + crossed + [swap(far, "c")]
    )

    from_sibling = swap(g_sib, "c")
    doc = sum_of_four(doc, ("z", "xl", "c"), 32, 4, 1)
    part = (g_own.astype(F32) + from_sibling.astype(F32)).astype(BF)
    part, doc = lax.optimization_barrier((part, doc))
    part = lax.all_to_all(part.reshape(2 * NZ, ROWS, 2 * HD), ("z", "xl"), 0, 0, tiled=True)
    grad_shape = jax.ShapeDtypeStruct((ROWS, 2, HD), BF)
    key_grad, value_grad = whole_call(
        grads_kernel, (grad_shape, grad_shape), part, limit=VMEM_LIMIT
    )

    gq_other = swap(gq_other, "xl")
    (query_grad,) = whole_call(
        query_grads_kernel, (jax.ShapeDtypeStruct((ROWS, 4, HD), BF),), gq_mine, gq_other,
        limit=VMEM_LIMIT,
    )

    doc = sum_of_four(doc, "h", 8, 2, 4)
    doc = sum_of_four(doc, ("xl", "h"), 16, 8, 1)
    doc = sum_of_four(doc, "z", 8, 2, 4)
    doc, key_grad = lax.optimization_barrier((doc, key_grad))
    doc_scores = doc[:DOCS, 0] / (count[:DOCS, 0] * (32 * HD))
    return (query_grad, key_grad, value_grad, doc_scores)


def solution(mesh):
    split = Mesh(mesh.devices.reshape(NZ, 2, 2, 8), ALL)
    ctx = ("z", "xl", "c")
    rows = P(ctx, "h", None)
    in_specs = (rows,) * 6 + (P("h", ctx), P(ctx))
    out_specs = (rows, rows, rows, P())
    return jax.shard_map(
        on_device, mesh=split, in_specs=in_specs, out_specs=out_specs, check_vma=False
    )
```

```python
import math

import jax
import jax.numpy as jnp
from jax import lax
from jax.experimental import pallas as pl
from jax.experimental.pallas import tpu as pltpu
from jax.sharding import Mesh, PartitionSpec as P

DOCS = 8
NZ = 8
FAR = NZ // 2
ROWS = 128
HD = 128
DR = 16
PIECE = ROWS + DR
CH = 2 * ROWS
MQ = 2 * CH
BK = 2 * CH
SCALE = 1.0 / 12.0
SCALE2 = SCALE * math.log2(math.e)
LOWEST = -1e30
ALL = ("z", "xl", "c", "h")
BF = jnp.bfloat16
F32 = jnp.float32
VMEM_LIMIT = 28 * 1024 * 1024


def dot(a, b):
    return lax.dot_general(a, b, (((1,), (0,)), ((), ())), preferred_element_type=F32)


def whole_call(kernel, out_shape, *arrays, limit=None):
    vmem = pl.BlockSpec(memory_space=pltpu.VMEM)
    return pl.pallas_call(
        kernel,
        out_shape=out_shape,
        in_specs=[vmem] * len(arrays),
        out_specs=(vmem,) * len(out_shape),
        compiler_params=pltpu.CompilerParams(vmem_limit_bytes=limit),
        cost_estimate=pl.CostEstimate(flops=0, bytes_accessed=1 << 20, transcendentals=0),
    )(*arrays)


def pack_keys_kernel(k, v, kt, vt, docs, kv_mine, kv_other):
    first = lax.axis_index("xl") == 0
    ids = jnp.broadcast_to(docs[...], (DR, HD)).astype(F32).astype(BF)
    for col, ref in enumerate((k, kt, v, vt)):
        a, b = ref[:, 0, :], ref[:, 1, :]
        lanes = pl.ds(col * HD, HD)
        kv_mine[pl.ds(0, ROWS), lanes] = jnp.where(first, a, b)
        kv_other[pl.ds(0, ROWS), lanes] = jnp.where(first, b, a)
        kv_mine[pl.ds(ROWS, DR), lanes] = ids
        kv_other[pl.ds(ROWS, DR), lanes] = ids


def pack_queries_kernel(q, qt, curv, q_mine, q_other):
    first = lax.axis_index("xl") == 0
    for h in range(2):
        for col, ref in enumerate((qt, q)):
            a, b = ref[:, h, :], ref[:, 2 + h, :]
            lanes = pl.ds((2 * h + col) * HD, HD)
            q_mine[pl.ds(0, ROWS), lanes] = jnp.where(first, a, b)
            q_other[pl.ds(0, ROWS), lanes] = jnp.where(first, b, a)
        a, b = curv[pl.ds(h, 1)], curv[pl.ds(2 + h, 1)]
        lanes = pl.ds(2 * h * HD, HD)
        for ref, row in ((q_mine, jnp.where(first, a, b)), (q_other, jnp.where(first, b, a))):
            row = jnp.broadcast_to(row, (DR, HD))
            line = lax.broadcasted_iota(jnp.int32, (DR, HD), 0)
            high = row.astype(BF).astype(F32)
            rest = row - high
            mid = rest.astype(BF).astype(F32)
            parts = jnp.where(line == 0, high, jnp.where(line == 1, mid, rest - mid))
            ref[pl.ds(ROWS, DR), lanes] = jnp.where(line < 3, parts, 0.0).astype(BF)
            ref[pl.ds(ROWS, DR), pl.ds((2 * h + 1) * HD, HD)] = jnp.zeros((DR, HD), BF)


def grads_kernel(parts, key_grad, value_grad):
    for head in range(2):
        total = parts[head].astype(F32)
        for z in range(1, NZ):
            total += parts[2 * z + head].astype(F32)
        key_grad[:, head, :] = total[:, :HD].astype(BF)
        value_grad[:, head, :] = total[:, HD:].astype(BF)


def query_grads_kernel(mine, other, query_grad):
    first = lax.axis_index("xl") == 0
    for h in range(2):
        query_grad[:, h, :] = jnp.where(first, mine[h], other[h])
        query_grad[:, 2 + h, :] = jnp.where(first, other[h], mine[h])


def rows_of(h, s):
    return (h * 2 + s) * ROWS


def masked(scores, xl, core):
    key = lax.broadcasted_iota(jnp.int32, scores.shape, 0)
    row = lax.broadcasted_iota(jnp.int32, scores.shape, 1) % CH
    row_xl = jnp.where(row >= ROWS, 1 - xl, xl)
    row_pos = row_xl * CH + core * ROWS + row % ROWS
    key_core = jnp.where(key >= CH, 1 - core, core)
    key = key % CH
    key_xl = jnp.where(key >= ROWS, 1 - xl, xl)
    key_pos = key_xl * CH + key_core * ROWS + key % ROWS
    return jnp.where(key_pos <= row_pos, scores, LOWEST)


def folded(x, combine):
    return combine(x.reshape(x.shape[0] // 8, 8, x.shape[1]), axis=0)


A0, B0, A1, B1, A2, B2, A3, B3, A4, B4 = range(10)
XA1, XB1, XA2, XB2, XA3, XB3, XA4, XB4 = range(10, 18)
NS = 18
BLOCKS = ((A0, B0), (A1, B1), (A2, B2), (A3, B3), None, (XA3, XB3), (XA2, XB2), (XA1, XB1))


def pieces_of(n):
    if n == FAR:
        return [(A4, 0), (B4, 0), (XA4, 0), (XB4, 0)]
    out = []
    for side in range(2):
        for at in BLOCKS[n]:
            out.append((at, PIECE * (1 - side if at >= XA1 else side)))
    return out


def attention_kernel(*refs):
    q_refs = refs[:2]
    sources = refs[2 : 2 + NS]
    refs = refs[2 + NS :]
    gq_mine, gq_other, g_own, g_sib, doc_ref, count_ref = refs[:6]
    q_t, q_n, score, acc_v, acc_t, cot_t, cot_n, stat, tops, tots, sprs, doc_acc = refs[6:]
    z = lax.axis_index("z")
    xl = lax.axis_index("xl")
    core = lax.axis_index("c")

    def keys(n, first, last):
        return jnp.concatenate(
            [
                sources[at][row : row + ROWS, first * HD : last * HD]
                for at, row in pieces_of(n)
            ],
            axis=0,
        )

    def onehot(piece):
        at, row = piece
        ids = sources[at][row + ROWS : row + PIECE, :HD].astype(F32).astype(jnp.int32)
        names = lax.broadcasted_iota(jnp.int32, (DR, ROWS), 0)
        return jnp.where(ids == names, 1.0, 0.0)

    def place(n):
        return jnp.where(core == 0, n, NZ - n) if n else 0

    def before(block):
        for n in range(1, NZ):
            pl.when(z >= place(n))(lambda n=n: block(n))

    curv = []
    for h in range(2):
        for s in range(2):
            q = q_refs[s]
            x = q[:ROWS, 2 * h * HD : 2 * (h + 1) * HD]
            q_n[pl.ds(rows_of(h, s), ROWS)] = x
            q_t[:, pl.ds(rows_of(h, s), ROWS)] = x.T
            line = q[ROWS:, 2 * h * HD : (2 * h + 1) * HD].astype(F32)
            curv.append(jnp.sum(line, axis=0, keepdims=True))
    curv = jnp.concatenate(curv, axis=1)

    def scores_of(d, diagonal):
        s = dot(keys(d, 0, 1), q_t[HD:, :]) * SCALE2
        if diagonal:
            s = masked(s, xl, core)
        score[d] = s
        top = folded(s, jnp.max)
        tops[...] = top if diagonal else jnp.maximum(tops[...], top)

    scores_of(0, True)
    before(lambda d: scores_of(d, False))
    top = jnp.max(tops[...], axis=0, keepdims=True)
    stat[0:1, :] = top

    def forward(d, diagonal):
        values_t = keys(d, 2, 4).T
        slope = dot(keys(d, 0, 2), q_t[...])
        e = jnp.exp2(score[d] - stat[0:1, :])
        f = e * slope
        part_v = dot(values_t, e.astype(BF))
        part_t = dot(values_t[:HD], f.astype(BF))
        tot, spr = folded(e, jnp.sum), folded(f, jnp.sum)
        if diagonal:
            acc_v[...], acc_t[...], tots[...], sprs[...] = part_v, part_t, tot, spr
        else:
            acc_v[...] += part_v
            acc_t[...] += part_t
            tots[...] += tot
            sprs[...] += spr

    forward(0, True)
    before(lambda d: forward(d, False))

    tot = jnp.sum(tots[...], axis=0, keepdims=True)
    spr = jnp.sum(sprs[...], axis=0, keepdims=True) * SCALE
    inv = 1.0 / tot
    out = acc_v[:HD, :] * inv
    out_tan = (acc_t[...] * SCALE + acc_v[HD:, :]) * inv - (spr * inv) * out
    cot = (curv * out_tan).astype(BF)
    cot_t[...] = cot
    cot_n[...] = cot.T
    stat[1:2, :] = stat[0:1, :] + jnp.log2(tot)
    stat[2:3, :] = jnp.sum(cot.astype(F32) * out, axis=0, keepdims=True)
    acc_t[...] = jnp.zeros((HD, MQ), F32)
    doc_acc[...] = jnp.zeros((DR, 2 * HD), F32)

    def by_document(hots, terms):
        hot = jnp.concatenate(hots, axis=1).astype(BF)
        high = terms.astype(BF)
        low = (terms - high.astype(F32)).astype(BF)
        return dot(hot, jnp.concatenate([high, low], axis=1))

    def backward(d):
        keys_t = keys(d, 0, 1).T
        p = jnp.exp2(score[d] - stat[1:2, :])
        push = dot(keys(d, 2, 3), cot_t[...])
        g = (p * (push - stat[2:3, :])).astype(BF)
        acc_t[...] += dot(keys_t, g)
        gk = dot(g, q_n[:, HD:]) * SCALE
        gv = dot(p.astype(BF), cot_n[...])
        terms = gk * keys(d, 1, 2).astype(F32) + gv * keys(d, 3, 4).astype(F32)
        for side, g_ref in enumerate((g_own, g_sib)):
            for s in range(2):
                at = side * CH + s * ROWS
                to_xl = xl if s == 0 else 1 - xl
                g_ref[z - place(d), to_xl, :, :HD] = gk[at : at + ROWS].astype(BF)
                g_ref[z - place(d), to_xl, :, HD:] = gv[at : at + ROWS].astype(BF)
        doc_acc[...] += by_document([onehot(p) for p in pieces_of(d)], terms)

    backward(0)
    before(backward)

    @pl.loop(z + 1, NZ)
    def _(to):
        g_own[to] = jnp.zeros((2, ROWS, 2 * HD), BF)
        g_sib[to] = jnp.zeros((2, ROWS, 2 * HD), BF)

    counts = sum(onehot(p) for n in range(NZ) for p in pieces_of(n))
    count_ref[...] = jnp.broadcast_to(jnp.sum(counts, axis=1, keepdims=True), (DR, ROWS))
    gq = (acc_t[...] * SCALE).T
    terms = gq * q_n[:, :HD].astype(F32)
    hots = [onehot(p) for p in pieces_of(0)[:2]]
    doc = doc_acc[...] + by_document(hots * 2, terms)
    for h in range(2):
        for s, ref in enumerate((gq_mine, gq_other)):
            ref[h] = gq[rows_of(h, s) : rows_of(h, s) + ROWS].astype(BF)
    doc_ref[...] = jnp.broadcast_to(jnp.sum(doc, axis=1, keepdims=True), (DR, HD))


def attention(q, sources):
    vmem = pl.BlockSpec(memory_space=pltpu.VMEM)
    gq_shape = jax.ShapeDtypeStruct((2, ROWS, HD), BF)
    g_shape = jax.ShapeDtypeStruct((NZ, 2, ROWS, 2 * HD), BF)
    line_shape = jax.ShapeDtypeStruct((DR, HD), F32)
    return pl.pallas_call(
        attention_kernel,
        out_shape=(gq_shape, gq_shape, g_shape, g_shape, line_shape, line_shape),
        in_specs=[vmem] * (2 + len(sources)),
        out_specs=(vmem,) * 6,
        scratch_shapes=[
            pltpu.VMEM((2 * HD, MQ), BF),
            pltpu.VMEM((MQ, 2 * HD), BF),
            pltpu.VMEM((NZ, BK, MQ), F32),
            pltpu.VMEM((2 * HD, MQ), F32),
            pltpu.VMEM((HD, MQ), F32),
            pltpu.VMEM((HD, MQ), BF),
            pltpu.VMEM((MQ, HD), BF),
            pltpu.VMEM((8, MQ), F32),
            pltpu.VMEM((8, MQ), F32),
            pltpu.VMEM((8, MQ), F32),
            pltpu.VMEM((8, MQ), F32),
            pltpu.VMEM((DR, 2 * HD), F32),
        ],
        compiler_params=pltpu.CompilerParams(vmem_limit_bytes=VMEM_LIMIT),
        cost_estimate=pl.CostEstimate(
            flops=8 * 2 * MQ * 4096 * 256, bytes_accessed=8 << 20, transcendentals=2 * MQ * 4096
        ),
    )(*q, *sources)


def swap(x, axis):
    return lax.ppermute(x, axis, [(0, 1), (1, 0)])


def around(x):
    pairs = [(2 * i + c, 2 * ((i + step) % NZ) + c) for i in range(NZ) for c, step in ((0, 1), (1, -1))]
    return lax.ppermute(x, ("z", "c"), pairs)


def bundle(x):
    return jnp.concatenate([x, swap(x, "c")], axis=0)


def sum_of_four(x, axes, size, one, two):
    got = [
        lax.ppermute(x, axes, [(i, i ^ m) for i in range(size)]) for m in (one, two, one ^ two)
    ]
    return (x + got[0]) + (got[1] + got[2])


def on_device(
    query_rows,
    key_rows,
    value_rows,
    query_tangent,
    key_tangent,
    value_tangent,
    curvature,
    documents,
):
    piece = jax.ShapeDtypeStruct((PIECE, 4 * HD), BF)
    kv_mine, kv_other = whole_call(
        pack_keys_kernel, (piece, piece),
        key_rows, value_rows, key_tangent, value_tangent, documents.reshape(1, ROWS),
    )
    kv_other = swap(kv_other, "xl")
    a = [bundle(kv_mine)]
    a[0], query_rows = lax.optimization_barrier((a[0], query_rows))
    a.append(around(a[0]))
    q_mine, q_other = whole_call(
        pack_queries_kernel, (piece, piece), query_rows, query_tangent, curvature
    )
    kv_other, q_other = lax.optimization_barrier((kv_other, q_other))
    b = [bundle(kv_other)]
    b.append(around(b[0]))
    crossed = []
    for k in range(1, FAR):
        late_a, b[k], q_other = lax.optimization_barrier((a[k], b[k], q_other))
        if k == 1:
            q_other = swap(q_other, "xl")
        crossed.append(swap(late_a, "c"))
        if k < FAR - 1:
            a.append(around(a[k]))
            late_b, _ = lax.optimization_barrier((b[k], a[k + 1]))
            crossed.append(swap(late_b, "c"))
            b.append(around(b[k]))
    crossed.append(swap(b[FAR - 1], "c"))
    far = [around(x[FAR - 1][:PIECE]) for x in (a, b)]
    native = [x for pair in zip(a, b) for x in pair]
    gq_mine, gq_other, g_own, g_sib, doc, count = attention(
        (q_mine, q_other), native + far + crossed + [swap(x, "c") for x in far]
    )

    from_sibling = swap(g_sib, "c")
    doc = sum_of_four(doc, ("z", "xl", "c"), 32, 4, 1)
    part = (g_own.astype(F32) + from_sibling.astype(F32)).astype(BF)
    part, doc = lax.optimization_barrier((part, doc))
    part = lax.all_to_all(part.reshape(2 * NZ, ROWS, 2 * HD), ("z", "xl"), 0, 0, tiled=True)
    grad_shape = jax.ShapeDtypeStruct((ROWS, 2, HD), BF)
    key_grad, value_grad = whole_call(
        grads_kernel, (grad_shape, grad_shape), part, limit=VMEM_LIMIT
    )

    gq_other = swap(gq_other, "xl")
    (query_grad,) = whole_call(
        query_grads_kernel, (jax.ShapeDtypeStruct((ROWS, 4, HD), BF),), gq_mine, gq_other,
        limit=VMEM_LIMIT,
    )

    doc = sum_of_four(doc, "h", 8, 2, 4)
    doc = sum_of_four(doc, ("xl", "h"), 16, 8, 1)
    doc = sum_of_four(doc, "z", 8, 2, 4)
    doc, key_grad = lax.optimization_barrier((doc, key_grad))
    doc_scores = doc[:DOCS, 0] / (count[:DOCS, 0] * (32 * HD))
    return (query_grad, key_grad, value_grad, doc_scores)


def solution(mesh):
    split = Mesh(mesh.devices.reshape(NZ, 2, 2, 8), ALL)
    ctx = ("z", "xl", "c")
    rows = P(ctx, "h", None)
    in_specs = (rows,) * 6 + (P("h", ctx), P(ctx))
    out_specs = (rows, rows, rows, P())
    return jax.shard_map(
        on_device, mesh=split, in_specs=in_specs, out_specs=out_specs, check_vma=False
    )
```
